1024 devices in a mesh: dp: 8 (over z), seq: 16 (over y, core), tensor: 8 (over x).
Axes of the slice: x: 8, y: 8, z: 8, core: 2. Of those that a mesh axis runs over, the one named last changes fastest.
Arguments:
- inputs: bfloat16 [8, 8192, 4096], P('dp', 'seq', 'tensor'), may hold values from -1.5 to 1.5
- logits: bfloat16 [8, 8192], P('dp', 'seq'), may hold values from -8 to 8
- cotangent: bfloat16 [8, 8192, 4096], P('dp', 'seq', 'tensor'), may hold values from -6 to 6
- attended: bfloat16 [8, 4096, 4096], P('dp', 'seq', 'tensor'), may hold values from -6 to 6
- out_weight: bfloat16 [4096, 4096], P('tensor'), may hold values from -0.09375 to 0.09375
- router_weight: float32 [4096], P('tensor'), may hold values from -6 to 6
- keep_route: int32 [8, 8192], P('dp', 'seq'), may hold values from 0 to 1, as said below
- shard_counts: int32 [8, 16], P('dp'), may hold values from 0 to 512, as said below
Outputs:
- attended_grad: bfloat16 [8, 4096, 4096], P('dp', 'seq', 'tensor')
- inputs_grad: bfloat16 [8, 8192, 4096], P('dp', 'seq', 'tensor')
- router_grad: float32 [4096], P('tensor')
The draws below stay inside these ranges and needn't reach their ends.
Inputs may be any that keep to these rules, and one draw needn't show every extreme that they name: `keep_route`: sequence b keeps exactly shard_counts[b, s] positions of its s-th block of 512 positions. `shard_counts`: each row sums to 4096; in every sequence some block keeps all its positions.
All inputs are finite; a program needn't handle non-finite values.
Results may differ from the reference program's by a relative error of at most 0.0013.
Values may be sent and summed in bfloat16 or wider, within the bound.
No kernel may reach another device: no remote copies, remote signals or barrier semaphores. Data moves between devices by JAX's collectives and lax.ppermute only.
A program may use at most 32 MiB of HBM per device.

```python
import math
import jax
import jax.numpy as jnp
from jax import lax

D = 4096
TOK_DEV = 512
KEEP_DEV = 256
LENGTH = 8192
KEPT = 4096
SEQS = 8
N_SEQ = 16


def split_counts(key):
    key = jax.random.fold_in(key, 11)
    keys = jax.random.split(key, SEQS)

    def one(single):
        first_key, second_key = jax.random.split(single)
        shifts = jax.random.randint(first_key, (N_SEQ // 2,), 0, KEEP_DEV + 1)
        shifts = shifts.at[0].set(KEEP_DEV)
        order = jax.random.permutation(second_key, N_SEQ)
        signed = jnp.concatenate([shifts, -shifts])
        return jnp.zeros((N_SEQ,), jnp.int32).at[order].set((KEEP_DEV + signed).astype(jnp.int32))
    return jax.vmap(one)(keys)


def draw_shard_counts(key, part):
    return split_counts(key)


def draw_keep_route(key, part):
    counts = split_counts(key)
    key = jax.random.fold_in(key, 5)
    keys = jax.random.split(key, SEQS * N_SEQ)
    orders = jax.vmap(lambda single: jax.random.permutation(single, TOK_DEV))(keys)
    keep = (orders < counts.reshape(SEQS * N_SEQ, 1)).astype(jnp.int32)
    return keep.reshape(SEQS, LENGTH)


def steps_of(key, extent, cuts, low, largest):
    gain, own = 1.0, jax.random.fold_in(key, 6)
    for axis_at, parts in cuts:
        heights = jnp.exp(jax.random.uniform(jax.random.fold_in(own, axis_at), (parts,), jnp.float32, low / len(cuts), largest / len(cuts)))
        gain = gain * jnp.repeat(heights, extent[axis_at] // parts).reshape([-1 if axis == axis_at else 1 for axis in range(len(extent))])
    return gain


def scatter_about(key, shape, width, most, shards=(), kind=jnp.bfloat16):
    entries = jax.random.normal(key, shape, jnp.float32) * width
    if len(shards) > 0:
        entries = steps_of(key, shape, shards, -0.22, 0.18) * entries
    return jnp.clip(entries, min=-most, max=most).astype(kind)


def setup_inputs(seed: int = 0) -> dict:
    streams_of = jax.random.split(jax.random.key(seed), 9)
    inputs = scatter_about(streams_of[0], (SEQS, LENGTH, D), 0.25, 1.5, ((0, 8), (1, 16), (2, 8)))
    logits = scatter_about(streams_of[1], (SEQS, LENGTH), 2.0, 8.0, ((0, 8), (1, 16)))
    cotangent = scatter_about(streams_of[2], (SEQS, LENGTH, D), 1.0, 6.0, ((0, 8), (1, 16), (2, 8)))
    attended = scatter_about(streams_of[3], (SEQS, KEPT, D), 1.0, 6.0, ((0, 8), (1, 16), (2, 8)))
    out_weight = scatter_about(streams_of[4], (D, D), D ** -0.5, 0.09375, ((0, 8),))
    router_weight = scatter_about(streams_of[5], (D,), 1.0, 6.0, ((0, 8),), jnp.float32)
    keep_route = draw_keep_route(jax.random.fold_in(streams_of[8], 71), 0)
    shard_counts = draw_shard_counts(jax.random.fold_in(streams_of[8], 71), 0)
    return {"inputs": inputs, "logits": logits, "cotangent": cotangent, "attended": attended, "out_weight": out_weight, "router_weight": router_weight, "keep_route": keep_route, "shard_counts": shard_counts}


def reference(inputs, logits, cotangent, attended, out_weight, router_weight, keep_route, shard_counts):
    scale = 1.0 / math.sqrt(D)

    def one(item):
        rows, logit, cot, att, keep, counts = item
        keep_f = keep.astype(jnp.float32)
        rate = jax.nn.sigmoid(logit.astype(jnp.float32))
        offsets = (jnp.cumsum(counts) - counts).astype(jnp.int32)
        local = (jnp.cumsum(keep.reshape(N_SEQ, TOK_DEV), axis=1) - 1).astype(jnp.int32)
        ranks = (offsets[:, None] + local).reshape(LENGTH)
        place = jnp.where(keep == 1, ranks % N_SEQ * KEEP_DEV + ranks // N_SEQ, KEPT).astype(jnp.int32)
        gathered = jnp.zeros((KEPT, D), jnp.bfloat16).at[place].set(cot, mode='drop')
        rate_kept = jnp.zeros((KEPT,), jnp.float32).at[place].set(rate, mode='drop')
        projected = jnp.dot(att, out_weight, preferred_element_type=jnp.float32)
        dots = lax.optimization_barrier(jnp.sum(gathered.astype(jnp.float32) * projected, axis=1))
        back = jnp.dot(gathered, out_weight.T, preferred_element_type=jnp.float32)
        att_grad = (rate_kept[:, None] * back).astype(jnp.bfloat16)
        dots_tok = dots[jnp.minimum(place, KEPT - 1).astype(jnp.int32)] * keep_f
        logit_grad = rate * (1.0 - rate) * dots_tok
        in_grad = (cot.astype(jnp.float32) + scale * logit_grad[:, None] * router_weight[None, :]).astype(jnp.bfloat16)
        partial_sum = scale * lax.optimization_barrier(jnp.sum(rows.astype(jnp.float32) * logit_grad[:, None], axis=0))
        return (att_grad, in_grad, partial_sum)
    att_grads, in_grads, partials = lax.map(one, (inputs, logits, cotangent, attended, keep_route, shard_counts))
    return (att_grads, in_grads, lax.optimization_barrier(jnp.sum(partials, axis=0)))
```

```python
import math

import jax
import jax.numpy as jnp
from jax import lax
from jax.sharding import PartitionSpec as P


def shards(
    inputs, logits, cotangent, attended, out_weight, router_weight, keep_route, shard_counts
):
    nseq = lax.axis_size("seq")
    here = lax.axis_index("seq")
    nten = lax.axis_size("tensor")
    column = lax.axis_index("tensor")
    batch, tok, width = cotangent.shape
    kept_rows = attended.shape[1]
    heads_width, model = out_weight.shape
    cap = tok // nseq
    scale = 1.0 / math.sqrt(model)

    rightward = [(i, (i + 1) % nten) for i in range(nten)]
    leftward = [(i, (i - 1) % nten) for i in range(nten)]

    def times(block, step):
        start = (column + step) % nten * width
        weight = lax.dynamic_slice(out_weight, (0, start), (heads_width, width))
        return lax.dot_general(
            block, weight, (((1,), (1,)), ((), ())), preferred_element_type=jnp.float32
        )

    own = cotangent.reshape(batch * tok, width)
    rows = batch * tok
    product = times(own, 0)
    from_left, from_right = own, own
    for step in range(1, nten // 2):
        from_left = lax.ppermute(from_left, "tensor", rightward)
        from_right = lax.ppermute(from_right, "tensor", leftward)
        product = product + times(from_left, -step) + times(from_right, step)
    upper = lax.ppermute(from_left[: rows // 2], "tensor", rightward)
    lower = lax.ppermute(from_right[rows // 2 :], "tensor", leftward)
    product = product + times(jnp.concatenate([upper, lower], axis=0), nten // 2)

    lanes = jnp.arange(nseq, dtype=jnp.int32)
    offsets = jnp.cumsum(shard_counts, axis=1) - shard_counts
    own_offset = jnp.sum(jnp.where(lanes[None, :] < here, shard_counts, 0), axis=1)
    local = jnp.cumsum(keep_route, axis=1) - 1
    ranks = own_offset[:, None] + local
    slot_ids = jnp.where(keep_route == 1, ranks % nseq * cap + local // nseq, -1)
    slot_table = (
        jnp.arange(tok, dtype=jnp.int32)[None, :, None] == slot_ids[:, None, :]
    ).astype(jnp.bfloat16)
    first = (here - offsets) % nseq
    order_in = first[:, :, None] + nseq * jnp.arange(cap, dtype=jnp.int32)[None, None, :]
    valid = order_in < shard_counts[:, :, None]
    positions = jnp.where(valid, (offsets[:, :, None] + order_in) // nseq, -1).reshape(batch, tok)
    place_table = (
        jnp.arange(kept_rows, dtype=jnp.int32)[None, :, None] == positions[:, None, :]
    ).astype(jnp.bfloat16)

    def exchange(slots):
        parts = slots.astype(jnp.bfloat16).reshape(batch, nseq, cap, slots.shape[2])
        moved = lax.all_to_all(parts, "seq", split_axis=1, concat_axis=1, tiled=True)
        return moved.reshape(batch, tok, slots.shape[2])

    att_slots = jnp.einsum(
        "bks,bkw->bsw", place_table, attended, preferred_element_type=jnp.float32
    )
    att_tok = jnp.einsum(
        "bst,bsw->btw", slot_table, exchange(att_slots), preferred_element_type=jnp.float32
    )

    back = product.reshape(batch, tok, heads_width)
    partial_dots = jnp.sum(att_tok * back, axis=2)
    copies = jnp.broadcast_to(partial_dots[None], (nten, batch, tok))
    dots = jnp.sum(lax.all_to_all(copies, "tensor", 0, 0, tiled=True), axis=0)
    rate = jax.nn.sigmoid(logits.astype(jnp.float32))
    logit_grad = rate * (1.0 - rate) * dots
    partial_sum = scale * jnp.sum(
        inputs.astype(jnp.float32) * logit_grad[:, :, None], axis=(0, 1)
    )
    group = lax.axis_size("dp") * nseq
    sums = jnp.broadcast_to(partial_sum[None], (group, width))
    router_grad = jnp.sum(lax.all_to_all(sums, ("dp", "seq"), 0, 0, tiled=True), axis=0)
    in_grad = (
        cotangent.astype(jnp.float32)
        + scale * logit_grad[:, :, None] * router_weight[None, None, :]
    ).astype(jnp.bfloat16)

    grad_tok = (rate[:, :, None] * back).astype(jnp.bfloat16)
    grad_slots = jnp.einsum(
        "bst,btw->bsw", slot_table, grad_tok, preferred_element_type=jnp.float32
    )
    att_grad = jnp.einsum(
        "bks,bsw->bkw", place_table, exchange(grad_slots), preferred_element_type=jnp.float32
    ).astype(jnp.bfloat16)
    return (att_grad, in_grad, router_grad)


def solution(mesh):
    in_specs = (
        P("dp", "seq", "tensor"),
        P("dp", "seq"),
        P("dp", "seq", "tensor"),
        P("dp", "seq", "tensor"),
        P("tensor", None),
        P("tensor"),
        P("dp", "seq"),
        P("dp", None),
    )
    out_specs = (P("dp", "seq", "tensor"), P("dp", "seq", "tensor"), P("tensor"))
    return jax.shard_map(shards, mesh=mesh, in_specs=in_specs, out_specs=out_specs, check_vma=False)
```

```python
import math

import jax
import jax.numpy as jnp
from jax import lax
from jax.sharding import PartitionSpec as P


def shards(
    inputs, logits, cotangent, attended, out_weight, router_weight, keep_route, shard_counts
):
    nseq = lax.axis_size("seq")
    here = lax.axis_index("seq")
    nten = lax.axis_size("tensor")
    column = lax.axis_index("tensor")
    batch, tok, width = cotangent.shape
    kept_rows = attended.shape[1]
    heads_width, model = out_weight.shape
    cap = tok // nseq
    scale = 1.0 / math.sqrt(model)

    rightward = [(i, (i + 1) % nten) for i in range(nten)]
    leftward = [(i, (i - 1) % nten) for i in range(nten)]

    def times(block, step):
        start = (column + step) % nten * width
        weight = lax.dynamic_slice(out_weight, (0, start), (heads_width, width))
        return lax.dot_general(
            block, weight, (((1,), (1,)), ((), ())), preferred_element_type=jnp.float32
        )

    own = cotangent.reshape(batch * tok, width)
    split = batch * tok // 2
    gathered = lax.all_gather(own[:split], "tensor", axis=1, tiled=True)
    from_left = from_right = own[split:]
    half = from_left.shape[0] // 2
    ringed = times(from_left, 0)
    for step in range(1, nten // 2):
        from_left = lax.ppermute(from_left, "tensor", rightward)
        from_right = lax.ppermute(from_right, "tensor", leftward)
        ringed = ringed + times(from_left, -step) + times(from_right, step)
    upper = lax.ppermute(from_left[:half], "tensor", rightward)
    lower = lax.ppermute(from_right[half:], "tensor", leftward)
    ringed = ringed + times(jnp.concatenate([upper, lower], axis=0), nten // 2)
    straight = lax.dot_general(
        gathered, out_weight, (((1,), (1,)), ((), ())), preferred_element_type=jnp.float32
    )

    lanes = jnp.arange(nseq, dtype=jnp.int32)
    offsets = jnp.cumsum(shard_counts, axis=1) - shard_counts
    own_offset = jnp.sum(jnp.where(lanes[None, :] < here, shard_counts, 0), axis=1)
    local = jnp.cumsum(keep_route, axis=1) - 1
    ranks = own_offset[:, None] + local
    slot_ids = jnp.where(keep_route == 1, ranks % nseq * cap + local // nseq, -1)
    slot_table = (
        jnp.arange(tok, dtype=jnp.int32)[None, :, None] == slot_ids[:, None, :]
    ).astype(jnp.bfloat16)
    first = (here - offsets) % nseq
    order_in = first[:, :, None] + nseq * jnp.arange(cap, dtype=jnp.int32)[None, None, :]
    valid = order_in < shard_counts[:, :, None]
    positions = jnp.where(valid, (offsets[:, :, None] + order_in) // nseq, -1).reshape(batch, tok)
    place_table = (
        jnp.arange(kept_rows, dtype=jnp.int32)[None, :, None] == positions[:, None, :]
    ).astype(jnp.bfloat16)

    def exchange(slots):
        parts = slots.astype(jnp.bfloat16).reshape(batch, nseq, cap, slots.shape[2])
        moved = lax.all_to_all(parts, "seq", split_axis=1, concat_axis=1, tiled=True)
        return moved.reshape(batch, tok, slots.shape[2])

    att_slots = jnp.einsum(
        "bks,bkw->bsw", place_table, attended, preferred_element_type=jnp.float32
    )
    att_tok = jnp.einsum(
        "bst,bsw->btw", slot_table, exchange(att_slots), preferred_element_type=jnp.float32
    )

    rate = jax.nn.sigmoid(logits.astype(jnp.float32))
    att_flat = att_tok.reshape(batch * tok, heads_width)
    rate_flat = rate.reshape(batch * tok, 1)
    partial_dots = jnp.concatenate(
        [
            jnp.sum(att_flat[:split] * straight, axis=1),
            jnp.sum(att_flat[split:] * ringed, axis=1),
        ]
    )
    grad_tok = jnp.concatenate(
        [
            (rate_flat[:split] * straight).astype(jnp.bfloat16),
            (rate_flat[split:] * ringed).astype(jnp.bfloat16),
        ]
    ).reshape(batch, tok, heads_width)
    grad_slots = jnp.einsum(
        "bst,btw->bsw", slot_table, grad_tok, preferred_element_type=jnp.float32
    ).astype(jnp.bfloat16)
    grad_slots, partial_dots = lax.optimization_barrier((grad_slots, partial_dots))
    grad_in = exchange(grad_slots)
    dots = lax.psum(partial_dots, "tensor").reshape(batch, tok)
    logit_grad = rate * (1.0 - rate) * dots
    partial_sum = scale * jnp.sum(
        inputs.astype(jnp.float32) * logit_grad[:, :, None], axis=(0, 1)
    )
    grad_in, partial_sum = lax.optimization_barrier((grad_in, partial_sum))

    group = lax.axis_size("dp") * nseq
    sums = jnp.broadcast_to(partial_sum[None], (group, width))
    router_grad = jnp.sum(lax.all_to_all(sums, ("dp", "seq"), 0, 0, tiled=True), axis=0)
    in_grad = (
        cotangent.astype(jnp.float32)
        + scale * logit_grad[:, :, None] * router_weight[None, None, :]
    ).astype(jnp.bfloat16)
    att_grad = jnp.einsum(
        "bks,bsw->bkw", place_table, grad_in, preferred_element_type=jnp.float32
    ).astype(jnp.bfloat16)
    return (att_grad, in_grad, router_grad)


def solution(mesh):
    in_specs = (
        P("dp", "seq", "tensor"),
        P("dp", "seq"),
        P("dp", "seq", "tensor"),
        P("dp", "seq", "tensor"),
        P("tensor", None),
        P("tensor"),
        P("dp", "seq"),
        P("dp", None),
    )
    out_specs = (P("dp", "seq", "tensor"), P("dp", "seq", "tensor"), P("tensor"))
    return jax.shard_map(shards, mesh=mesh, in_specs=in_specs, out_specs=out_specs, check_vma=False)
```

```python
import math

import jax
import jax.numpy as jnp
from jax import lax
from jax.sharding import PartitionSpec as P


def shards(
    inputs, logits, cotangent, attended, out_weight, router_weight, keep_route, shard_counts
):
    nseq = lax.axis_size("seq")
    here = lax.axis_index("seq")
    nten = lax.axis_size("tensor")
    column = lax.axis_index("tensor")
    batch, tok, width = cotangent.shape
    kept_rows = attended.shape[1]
    heads_width, model = out_weight.shape
    cap = tok // nseq
    scale = 1.0 / math.sqrt(model)

    rightward = [(i, (i + 1) % nten) for i in range(nten)]
    leftward = [(i, (i - 1) % nten) for i in range(nten)]

    def times(block, step):
        start = (column + step) % nten * width
        weight = lax.dynamic_slice(out_weight, (0, start), (heads_width, width))
        return lax.dot_general(
            block, weight, (((1,), (1,)), ((), ())), preferred_element_type=jnp.float32
        )

    lanes = jnp.arange(nseq, dtype=jnp.int32)
    offsets = jnp.cumsum(shard_counts, axis=1) - shard_counts
    own_offset = jnp.sum(jnp.where(lanes[None, :] < here, shard_counts, 0), axis=1)
    local = jnp.cumsum(keep_route, axis=1) - 1
    ranks = own_offset[:, None] + local
    slot_ids = jnp.where(keep_route == 1, ranks % nseq * cap + local // nseq, -1)
    slot_table = (
        jnp.arange(tok, dtype=jnp.int32)[None, :, None] == slot_ids[:, None, :]
    ).astype(jnp.bfloat16)
    first = (here - offsets) % nseq
    order_in = first[:, :, None] + nseq * jnp.arange(cap, dtype=jnp.int32)[None, None, :]
    valid = order_in < shard_counts[:, :, None]
    positions = jnp.where(valid, (offsets[:, :, None] + order_in) // nseq, -1).reshape(batch, tok)
    place_table = (
        jnp.arange(kept_rows, dtype=jnp.int32)[None, :, None] == positions[:, None, :]
    ).astype(jnp.bfloat16)

    def exchange(slots):
        parts = slots.reshape(batch, nseq, cap, slots.shape[2])
        moved = lax.all_to_all(parts, "seq", split_axis=1, concat_axis=1, tiled=True)
        return moved.reshape(batch, tok, slots.shape[2])

    own = cotangent.reshape(batch * tok, width)
    rows = batch * tok
    from_left, from_right = own, own
    product = times(own, 0)
    for step in range(1, nten // 2):
        from_left = lax.ppermute(from_left, "tensor", rightward)
        from_right = lax.ppermute(from_right, "tensor", leftward)
        if step == 1:
            attended, place_table, from_left, from_right, product = lax.optimization_barrier(
                (attended, place_table, from_left, from_right, product)
            )
            att_slots = jnp.einsum(
                "bks,bkw->bsw", place_table, attended, preferred_element_type=jnp.float32
            ).astype(jnp.bfloat16)
            att_in = exchange(att_slots)
        product = product + times(from_left, -step) + times(from_right, step)
    upper = lax.ppermute(from_left[: rows // 2], "tensor", rightward)
    lower = lax.ppermute(from_right[rows // 2 :], "tensor", leftward)
    product = product + times(jnp.concatenate([upper, lower], axis=0), nten // 2)
    att_tok = jnp.einsum("bst,bsw->btw", slot_table, att_in, preferred_element_type=jnp.float32)

    rate = jax.nn.sigmoid(logits.astype(jnp.float32))
    back = product.reshape(batch, tok, heads_width)
    partial_dots = jnp.sum(att_tok * back, axis=2)
    grad_tok = (rate[:, :, None] * back).astype(jnp.bfloat16)
    grad_slots = jnp.einsum(
        "bst,btw->bsw", slot_table, grad_tok, preferred_element_type=jnp.float32
    ).astype(jnp.bfloat16)
    grad_slots, partial_dots = lax.optimization_barrier((grad_slots, partial_dots))
    grad_in = exchange(grad_slots)
    dots = lax.psum(partial_dots, "tensor")
    logit_grad = rate * (1.0 - rate) * dots
    partial_sum = scale * jnp.sum(
        inputs.astype(jnp.float32) * logit_grad[:, :, None], axis=(0, 1)
    )
    grad_in, partial_sum = lax.optimization_barrier((grad_in, partial_sum))

    group = lax.axis_size("dp") * nseq
    sums = jnp.broadcast_to(partial_sum[None], (group, width))
    router_grad = jnp.sum(lax.all_to_all(sums, ("dp", "seq"), 0, 0, tiled=True), axis=0)
    in_grad = (
        cotangent.astype(jnp.float32)
        + scale * logit_grad[:, :, None] * router_weight[None, None, :]
    ).astype(jnp.bfloat16)
    att_grad = jnp.einsum(
        "bks,bsw->bkw", place_table, grad_in, preferred_element_type=jnp.float32
    ).astype(jnp.bfloat16)
    return (att_grad, in_grad, router_grad)


def solution(mesh):
    in_specs = (
        P("dp", "seq", "tensor"),
        P("dp", "seq"),
        P("dp", "seq", "tensor"),
        P("dp", "seq", "tensor"),
        P("tensor", None),
        P("tensor"),
        P("dp", "seq"),
        P("dp", None),
    )
    out_specs = (P("dp", "seq", "tensor"), P("dp", "seq", "tensor"), P("tensor"))
    return jax.shard_map(shards, mesh=mesh, in_specs=in_specs, out_specs=out_specs, check_vma=False)
```

```python
import math

import jax
import jax.numpy as jnp
from jax import lax
from jax.sharding import PartitionSpec as P


def shards(
    inputs, logits, cotangent, attended, out_weight, router_weight, keep_route, shard_counts
):
    nseq = lax.axis_size("seq")
    here = lax.axis_index("seq")
    nten = lax.axis_size("tensor")
    column = lax.axis_index("tensor")
    batch, tok, width = cotangent.shape
    kept_rows = attended.shape[1]
    heads_width, model = out_weight.shape
    cap = tok // nseq
    scale = 1.0 / math.sqrt(model)

    flip = 1 - 2 * (here % 2)

    def turn(block, way):
        pairs = [
            (s * nten + i, s * nten + (i + (way if s % 2 == 0 else -way)) % nten)
            for s in range(nseq)
            for i in range(nten)
        ]
        return lax.ppermute(block, ("seq", "tensor"), pairs)

    def times(block, step):
        start = (column + step * flip) % nten * width
        weight = lax.dynamic_slice(out_weight, (0, start), (heads_width, width))
        return lax.dot_general(
            block, weight, (((1,), (1,)), ((), ())), preferred_element_type=jnp.float32
        )

    lanes = jnp.arange(nseq, dtype=jnp.int32)
    offsets = jnp.cumsum(shard_counts, axis=1) - shard_counts
    own_offset = jnp.sum(jnp.where(lanes[None, :] < here, shard_counts, 0), axis=1)
    local = jnp.cumsum(keep_route, axis=1) - 1
    ranks = own_offset[:, None] + local
    slot_ids = jnp.where(keep_route == 1, ranks % nseq * cap + local // nseq, -1)
    slot_table = (
        jnp.arange(tok, dtype=jnp.int32)[None, :, None] == slot_ids[:, None, :]
    ).astype(jnp.bfloat16)
    start = (here - offsets) % nseq
    order_in = start[:, :, None] + nseq * jnp.arange(cap, dtype=jnp.int32)[None, None, :]
    valid = order_in < shard_counts[:, :, None]
    positions = jnp.where(valid, (offsets[:, :, None] + order_in) // nseq, -1).reshape(batch, tok)
    place_table = (
        jnp.arange(kept_rows, dtype=jnp.int32)[None, :, None] == positions[:, None, :]
    ).astype(jnp.bfloat16)

    def exchange(slots):
        parts = slots.reshape(batch, nseq, cap, slots.shape[2])
        moved = lax.all_to_all(parts, "seq", split_axis=1, concat_axis=1, tiled=True)
        return moved.reshape(batch, tok, slots.shape[2])

    own = cotangent.reshape(batch * tok, width)
    rows = batch * tok
    first_in, second_in = own, own
    product = times(own, 0)
    for step in range(1, nten // 2):
        first_in = turn(first_in, 1)
        second_in = turn(second_in, -1)
        if step == 1:
            attended, place_table, first_in = lax.optimization_barrier(
                (attended, place_table, first_in)
            )
            att_slots = jnp.einsum(
                "bks,bkw->bsw", place_table, attended, preferred_element_type=jnp.float32
            ).astype(jnp.bfloat16)
            att_in = exchange(att_slots)
        product = product + times(first_in, -step) + times(second_in, step)
    upper = turn(first_in[: rows // 2], 1)
    lower = turn(second_in[rows // 2 :], -1)
    product = product + times(jnp.concatenate([upper, lower], axis=0), nten // 2)
    att_tok = jnp.einsum("bst,bsw->btw", slot_table, att_in, preferred_element_type=jnp.float32)

    rate = jax.nn.sigmoid(logits.astype(jnp.float32))
    back = product.reshape(batch, tok, heads_width)
    partial_dots = jnp.sum(att_tok * back, axis=2)
    grad_tok = (rate[:, :, None] * back).astype(jnp.bfloat16)
    grad_slots = jnp.einsum(
        "bst,btw->bsw", slot_table, grad_tok, preferred_element_type=jnp.float32
    ).astype(jnp.bfloat16)
    grad_slots, partial_dots = lax.optimization_barrier((grad_slots, partial_dots))
    grad_in = exchange(grad_slots)
    dots = lax.psum(partial_dots, "tensor")
    logit_grad = rate * (1.0 - rate) * dots
    partial_sum = scale * jnp.sum(
        inputs.astype(jnp.float32) * logit_grad[:, :, None], axis=(0, 1)
    )
    grad_in, partial_sum = lax.optimization_barrier((grad_in, partial_sum))

    group = lax.axis_size("dp") * nseq
    sums = jnp.broadcast_to(partial_sum[None], (group, width))
    router_grad = jnp.sum(lax.all_to_all(sums, ("dp", "seq"), 0, 0, tiled=True), axis=0)
    in_grad = (
        cotangent.astype(jnp.float32)
        + scale * logit_grad[:, :, None] * router_weight[None, None, :]
    ).astype(jnp.bfloat16)
    att_grad = jnp.einsum(
        "bks,bsw->bkw", place_table, grad_in, preferred_element_type=jnp.float32
    ).astype(jnp.bfloat16)
    return (att_grad, in_grad, router_grad)


def solution(mesh):
    in_specs = (
        P("dp", "seq", "tensor"),
        P("dp", "seq"),
        P("dp", "seq", "tensor"),
        P("dp", "seq", "tensor"),
        P("tensor", None),
        P("tensor"),
        P("dp", "seq"),
        P("dp", None),
    )
    out_specs = (P("dp", "seq", "tensor"), P("dp", "seq", "tensor"), P("tensor"))
    return jax.shard_map(shards, mesh=mesh, in_specs=in_specs, out_specs=out_specs, check_vma=False)
```

```python
import functools
import math

import jax
import jax.numpy as jnp
from jax import lax
from jax.experimental import pallas as pl
from jax.experimental.pallas import tpu as pltpu
from jax.sharding import PartitionSpec as P


VMEM = pl.BlockSpec(memory_space=pltpu.VMEM)
SMEM = pl.BlockSpec(memory_space=pltpu.SMEM)
PARAMS = pltpu.CompilerParams(vmem_limit_bytes=32 * 1024 * 1024)


def pack_kernel(here_ref, counts_ref, keep_ref, att_ref, slots_ref, ids_ref, places_ref):
    nseq = counts_ref.shape[1]
    tok = keep_ref.shape[1]
    kept_rows = att_ref.shape[0]
    cap = tok // nseq
    seq_bits, cap_bits = nseq.bit_length() - 1, cap.bit_length() - 1
    here = here_ref[0]
    lane = lax.broadcasted_iota(jnp.int32, (1, tok), 1)
    block = lane >> cap_bits
    offset, own_offset = jnp.int32(0), jnp.int32(0)
    offsets = jnp.zeros((1, tok), jnp.int32)
    counts = jnp.zeros((1, tok), jnp.int32)
    for j in range(nseq):
        count = counts_ref[0, j]
        offsets = jnp.where(block == j, offset, offsets)
        counts = jnp.where(block == j, count, counts)
        own_offset = own_offset + jnp.where(j < here, count, 0)
        offset = offset + count
    order_in = ((here - offsets) & (nseq - 1)) + nseq * (lane & (cap - 1))
    places = jnp.where(order_in < counts, (offsets + order_in) >> seq_bits, -1)
    places_ref[...] = places

    keep = keep_ref[...]
    flags = jnp.broadcast_to(keep.astype(jnp.float32), (16, tok)).astype(jnp.bfloat16)
    upto = lax.broadcasted_iota(jnp.int32, (tok, tok), 0) <= lax.broadcasted_iota(
        jnp.int32, (tok, tok), 1
    )
    upto = jnp.where(upto, 1.0, 0.0).astype(jnp.bfloat16)
    sums = jnp.dot(flags, upto, preferred_element_type=jnp.float32)
    local = sums[0:1].astype(jnp.int32) - 1
    ranks = own_offset + local
    slot = (ranks & (nseq - 1)) * cap + (local >> seq_bits)
    ids_ref[...] = jnp.where(keep == 1, slot, -1)

    table = lax.broadcasted_iota(jnp.int32, (kept_rows, tok), 0) == places
    table = jnp.where(table, 1.0, 0.0).astype(jnp.bfloat16)
    slots_ref[...] = lax.dot_general(
        table, att_ref[...], (((0,), (0,)), ((), ())), preferred_element_type=jnp.float32
    ).astype(jnp.bfloat16)


def finish_kernel(att_ref, ids_ref, rate_ref, back_ref, slots_ref, dots_ref):
    tok = ids_ref.shape[1]
    table = lax.broadcasted_iota(jnp.int32, (tok, tok), 0) == ids_ref[...]
    table = jnp.where(table, 1.0, 0.0).astype(jnp.bfloat16)
    att_tok = lax.dot_general(
        table, att_ref[...], (((0,), (0,)), ((), ())), preferred_element_type=jnp.float32
    )
    back = back_ref[...]
    column = jnp.sum(att_tok * back, axis=1, keepdims=True)
    dots_ref[...] = jnp.broadcast_to(column, (tok, 128)).T[0:1]
    rate = jnp.broadcast_to(rate_ref[...], (128, tok)).T[:, 0:1]
    grad = (rate * back).astype(jnp.bfloat16)
    slots_ref[...] = jnp.dot(table, grad, preferred_element_type=jnp.float32).astype(jnp.bfloat16)


def router_kernel(scale, dots_ref, rate_ref, inputs_ref, copies_ref, grad_ref):
    rate = rate_ref[...]
    grad = rate * (1.0 - rate) * dots_ref[...]
    grad_ref[...] = grad
    high = grad.astype(jnp.bfloat16).astype(jnp.float32)
    middle = (grad - high).astype(jnp.bfloat16).astype(jnp.float32)
    low = grad - high - middle
    row = lax.broadcasted_iota(jnp.int32, (16, grad.shape[1]), 0)
    parts = jnp.where(row == 0, high, jnp.where(row == 1, middle, jnp.where(row == 2, low, 0.0)))
    sums = jnp.dot(
        parts.astype(jnp.bfloat16), inputs_ref[...], preferred_element_type=jnp.float32
    )
    total = scale * jnp.sum(sums, axis=0, keepdims=True)
    copies_ref[...] = jnp.broadcast_to(total[None], copies_ref.shape)


def shards(
    inputs, logits, cotangent, attended, out_weight, router_weight, keep_route, shard_counts
):
    nseq = lax.axis_size("seq")
    here = lax.axis_index("seq")
    nten = lax.axis_size("tensor")
    column = lax.axis_index("tensor")
    batch, tok, width = cotangent.shape
    kept_rows = attended.shape[1]
    heads_width, model = out_weight.shape
    cap = tok // nseq
    scale = 1.0 / math.sqrt(model)

    flip = 1 - 2 * (here % 2)

    def turn(block, way):
        pairs = [
            (s * nten + i, s * nten + (i + (way if s % 2 == 0 else -way)) % nten)
            for s in range(nseq)
            for i in range(nten)
        ]
        return lax.ppermute(block, ("seq", "tensor"), pairs)

    def times(block, step):
        start = (column + step * flip) % nten * width
        weight = lax.dynamic_slice(out_weight, (0, start), (heads_width, width))
        return lax.dot_general(
            block, weight, (((1,), (1,)), ((), ())), preferred_element_type=jnp.float32
        )

    slots_shape = jax.ShapeDtypeStruct((tok, heads_width), jnp.bfloat16)
    row_shape = jax.ShapeDtypeStruct((1, tok), jnp.int32)
    att_slots, slot_ids, places = pl.pallas_call(
        pack_kernel,
        out_shape=(slots_shape, row_shape, row_shape),
        in_specs=[SMEM, SMEM, VMEM, VMEM],
        out_specs=(VMEM, VMEM, VMEM),
        compiler_params=PARAMS,
        cost_estimate=pl.CostEstimate(
            flops=2 * tok * kept_rows * heads_width, bytes_accessed=2**20, transcendentals=0
        ),
    )(here.reshape(1), shard_counts, keep_route, attended[0])

    def exchange(slots):
        parts = slots.reshape(nseq, cap, slots.shape[1])
        moved = lax.all_to_all(parts, "seq", split_axis=0, concat_axis=0, tiled=True)
        return moved.reshape(tok, slots.shape[1])

    att_in = exchange(att_slots)

    own = cotangent[0]
    first_in, second_in = own, own
    product = None
    for step in range(1, nten // 2):
        first_in = turn(first_in, 1)
        second_in = turn(second_in, -1)
        if step == 1:
            own, first_in = lax.optimization_barrier((own, first_in))
            product = times(own, 0)
        product = product + times(first_in, -step) + times(second_in, step)
    upper = turn(first_in[: tok // 2], 1)
    lower = turn(second_in[tok // 2 :], -1)
    product = product + times(jnp.concatenate([upper, lower], axis=0), nten // 2)

    rate = jax.nn.sigmoid(logits.astype(jnp.float32))
    grad_slots, partial_dots = pl.pallas_call(
        finish_kernel,
        out_shape=(slots_shape, jax.ShapeDtypeStruct((1, tok), jnp.float32)),
        in_specs=[VMEM] * 4,
        out_specs=(VMEM, VMEM),
        compiler_params=PARAMS,
        cost_estimate=pl.CostEstimate(
            flops=4 * tok * tok * heads_width, bytes_accessed=2**21, transcendentals=0
        ),
    )(att_in, slot_ids, rate, product)
    grad_in = exchange(grad_slots)
    dots = lax.psum(partial_dots, "tensor")
    group = lax.axis_size("dp") * nseq
    copies, logit_grad = pl.pallas_call(
        functools.partial(router_kernel, scale),
        out_shape=(
            jax.ShapeDtypeStruct((group, 1, width), jnp.float32),
            jax.ShapeDtypeStruct((1, tok), jnp.float32),
        ),
        in_specs=[VMEM] * 3,
        out_specs=(VMEM, VMEM),
        compiler_params=PARAMS,
        cost_estimate=pl.CostEstimate(
            flops=32 * tok * width, bytes_accessed=2**20, transcendentals=0
        ),
    )(dots, rate, inputs[0])
    grad_in, copies = lax.optimization_barrier((grad_in, copies))

    router_grad = jnp.sum(lax.all_to_all(copies, ("dp", "seq"), 0, 0, tiled=True), axis=(0, 1))
    in_grad = (
        cotangent.astype(jnp.float32)
        + scale * logit_grad[:, :, None] * router_weight[None, None, :]
    ).astype(jnp.bfloat16)
    place_table = (
        jnp.arange(kept_rows, dtype=jnp.int32)[:, None] == places
    ).astype(jnp.bfloat16)
    att_grad = jnp.dot(place_table, grad_in, preferred_element_type=jnp.float32)
    att_grad = att_grad.astype(jnp.bfloat16)[None]
    return (att_grad, in_grad, router_grad)


def solution(mesh):
    in_specs = (
        P("dp", "seq", "tensor"),
        P("dp", "seq"),
        P("dp", "seq", "tensor"),
        P("dp", "seq", "tensor"),
        P("tensor", None),
        P("tensor"),
        P("dp", "seq"),
        P("dp", None),
    )
    out_specs = (P("dp", "seq", "tensor"), P("dp", "seq", "tensor"), P("tensor"))
    return jax.shard_map(shards, mesh=mesh, in_specs=in_specs, out_specs=out_specs, check_vma=False)
```

```python
import functools
import math

import jax
import jax.numpy as jnp
from jax import lax
from jax.experimental import pallas as pl
from jax.experimental.pallas import tpu as pltpu
from jax.sharding import PartitionSpec as P


VMEM = pl.BlockSpec(memory_space=pltpu.VMEM)
SMEM = pl.BlockSpec(memory_space=pltpu.SMEM)
PARAMS = pltpu.CompilerParams(vmem_limit_bytes=32 * 1024 * 1024)


def pack_kernel(
    here_ref, counts_ref, keep_ref, att_any, slots_ref, ids_ref, places_ref, att_ref, att_sem
):
    fetch = pltpu.make_async_copy(att_any, att_ref, att_sem)
    fetch.start()
    nseq = counts_ref.shape[1]
    tok = keep_ref.shape[1]
    kept_rows = att_ref.shape[0]
    cap = tok // nseq
    seq_bits, cap_bits = nseq.bit_length() - 1, cap.bit_length() - 1
    here = here_ref[0]
    lane = lax.broadcasted_iota(jnp.int32, (1, tok), 1)
    block = lane >> cap_bits
    offset, own_offset = jnp.int32(0), jnp.int32(0)
    offsets = jnp.zeros((1, tok), jnp.int32)
    counts = jnp.zeros((1, tok), jnp.int32)
    for j in range(nseq):
        count = counts_ref[0, j]
        offsets = jnp.where(block == j, offset, offsets)
        counts = jnp.where(block == j, count, counts)
        own_offset = own_offset + jnp.where(j < here, count, 0)
        offset = offset + count
    order_in = ((here - offsets) & (nseq - 1)) + nseq * (lane & (cap - 1))
    places = jnp.where(order_in < counts, (offsets + order_in) >> seq_bits, -1)
    places_ref[...] = places

    keep = keep_ref[...]
    flags = jnp.broadcast_to(keep.astype(jnp.float32), (16, tok)).astype(jnp.bfloat16)
    upto = lax.broadcasted_iota(jnp.int32, (tok, tok), 0) <= lax.broadcasted_iota(
        jnp.int32, (tok, tok), 1
    )
    upto = jnp.where(upto, 1.0, 0.0).astype(jnp.bfloat16)
    sums = jnp.dot(flags, upto, preferred_element_type=jnp.float32)
    local = sums[0:1].astype(jnp.int32) - 1
    ranks = own_offset + local
    slot = (ranks & (nseq - 1)) * cap + (local >> seq_bits)
    ids_ref[...] = jnp.where(keep == 1, slot, -1)

    table = lax.broadcasted_iota(jnp.int32, (kept_rows, tok), 0) == places
    table = jnp.where(table, 1.0, 0.0).astype(jnp.bfloat16)
    fetch.wait()
    slots_ref[...] = lax.dot_general(
        table, att_ref[...], (((0,), (0,)), ((), ())), preferred_element_type=jnp.float32
    ).astype(jnp.bfloat16)


def rate_of(logits_ref):
    return jax.nn.sigmoid(logits_ref[...].astype(jnp.float32))


def finish_kernel(att_ref, ids_ref, logits_ref, back_ref, slots_ref, dots_ref):
    tok = ids_ref.shape[1]
    table = lax.broadcasted_iota(jnp.int32, (tok, tok), 0) == ids_ref[...]
    table = jnp.where(table, 1.0, 0.0).astype(jnp.bfloat16)
    att_tok = lax.dot_general(
        table, att_ref[...], (((0,), (0,)), ((), ())), preferred_element_type=jnp.float32
    )
    back = back_ref[...]
    column = jnp.sum(att_tok * back, axis=1, keepdims=True)
    dots_ref[...] = jnp.broadcast_to(column, (tok, 128)).T[0:1]
    rate = jnp.broadcast_to(rate_of(logits_ref), (128, tok)).T[:, 0:1]
    grad = (rate * back).astype(jnp.bfloat16)
    slots_ref[...] = jnp.dot(table, grad, preferred_element_type=jnp.float32).astype(jnp.bfloat16)


def router_kernel(scale, dots_ref, logits_ref, inputs_ref, copies_ref, grad_ref):
    rate = rate_of(logits_ref)
    grad = rate * (1.0 - rate) * dots_ref[...]
    grad_ref[...] = grad
    high = grad.astype(jnp.bfloat16).astype(jnp.float32)
    middle = (grad - high).astype(jnp.bfloat16).astype(jnp.float32)
    low = grad - high - middle
    row = lax.broadcasted_iota(jnp.int32, (16, grad.shape[1]), 0)
    parts = jnp.where(row == 0, high, jnp.where(row == 1, middle, jnp.where(row == 2, low, 0.0)))
    sums = jnp.dot(
        parts.astype(jnp.bfloat16), inputs_ref[...], preferred_element_type=jnp.float32
    )
    total = scale * jnp.sum(sums, axis=0, keepdims=True)
    copies_ref[...] = jnp.broadcast_to(total[None], copies_ref.shape)


def shards(
    inputs, logits, cotangent, attended, out_weight, router_weight, keep_route, shard_counts
):
    nseq = lax.axis_size("seq")
    here = lax.axis_index("seq")
    nten = lax.axis_size("tensor")
    column = lax.axis_index("tensor")
    batch, tok, width = cotangent.shape
    kept_rows = attended.shape[1]
    heads_width, model = out_weight.shape
    cap = tok // nseq
    scale = 1.0 / math.sqrt(model)

    flip = 1 - 2 * (here % 2)

    def turn(block, way):
        pairs = [
            (s * nten + i, s * nten + (i + (way if s % 2 == 0 else -way)) % nten)
            for s in range(nseq)
            for i in range(nten)
        ]
        return lax.ppermute(block, ("seq", "tensor"), pairs)

    def times(block, step):
        start = (column + step * flip) % nten * width
        weight = lax.dynamic_slice(out_weight, (0, start), (heads_width, width))
        return lax.dot_general(
            block, weight, (((1,), (1,)), ((), ())), preferred_element_type=jnp.float32
        )

    slots_shape = jax.ShapeDtypeStruct((tok, heads_width), jnp.bfloat16)
    row_shape = jax.ShapeDtypeStruct((1, tok), jnp.int32)
    att_slots, slot_ids, places = pl.pallas_call(
        pack_kernel,
        out_shape=(slots_shape, row_shape, row_shape),
        in_specs=[SMEM, SMEM, VMEM, pl.BlockSpec(memory_space=pl.ANY)],
        out_specs=(VMEM, VMEM, VMEM),
        scratch_shapes=[
            pltpu.VMEM((kept_rows, heads_width), jnp.bfloat16),
            pltpu.SemaphoreType.DMA,
        ],
        compiler_params=PARAMS,
        cost_estimate=pl.CostEstimate(
            flops=2 * tok * kept_rows * heads_width, bytes_accessed=2**20, transcendentals=0
        ),
    )(here.reshape(1), shard_counts, keep_route, attended[0])

    def exchange(slots):
        parts = slots.reshape(nseq, cap, slots.shape[1])
        moved = lax.all_to_all(parts, "seq", split_axis=0, concat_axis=0, tiled=True)
        return moved.reshape(tok, slots.shape[1])

    att_in = exchange(att_slots)

    own = cotangent[0]
    first_in, second_in = own, own
    blocks = [(own, 0)]
    for step in range(1, nten // 2):
        first_in = turn(first_in, 1)
        second_in = turn(second_in, -1)
        if step == 2:
            waiting = tuple(block for block, _ in blocks)
            waiting, second_in = lax.optimization_barrier((waiting, second_in))
            blocks = [(block, way) for block, (_, way) in zip(waiting, blocks)]
        blocks += [(first_in, -step), (second_in, step)]
    product = sum(times(block, way) for block, way in blocks)
    last_in = turn(first_in, 1)
    product = product + times(last_in, nten // 2)

    grad_slots, partial_dots = pl.pallas_call(
        finish_kernel,
        out_shape=(slots_shape, jax.ShapeDtypeStruct((1, tok), jnp.float32)),
        in_specs=[VMEM] * 4,
        out_specs=(VMEM, VMEM),
        compiler_params=PARAMS,
        cost_estimate=pl.CostEstimate(
            flops=4 * tok * tok * heads_width, bytes_accessed=2**21, transcendentals=0
        ),
    )(att_in, slot_ids, logits, product)
    grad_in = exchange(grad_slots)
    dots = lax.psum(partial_dots, "tensor")
    group = lax.axis_size("dp") * nseq
    copies, logit_grad = pl.pallas_call(
        functools.partial(router_kernel, scale),
        out_shape=(
            jax.ShapeDtypeStruct((group, 1, width), jnp.float32),
            jax.ShapeDtypeStruct((1, tok), jnp.float32),
        ),
        in_specs=[VMEM] * 3,
        out_specs=(VMEM, VMEM),
        compiler_params=PARAMS,
        cost_estimate=pl.CostEstimate(
            flops=32 * tok * width, bytes_accessed=2**20, transcendentals=0
        ),
    )(dots, logits, inputs[0])
    grad_in, copies = lax.optimization_barrier((grad_in, copies))

    router_grad = jnp.sum(lax.all_to_all(copies, ("dp", "seq"), 0, 0, tiled=True), axis=(0, 1))
    in_grad = (
        cotangent.astype(jnp.float32)
        + scale * logit_grad[:, :, None] * router_weight[None, None, :]
    ).astype(jnp.bfloat16)
    place_table = (
        jnp.arange(kept_rows, dtype=jnp.int32)[:, None] == places
    ).astype(jnp.bfloat16)
    att_grad = jnp.dot(place_table, grad_in, preferred_element_type=jnp.float32)
    att_grad = att_grad.astype(jnp.bfloat16)[None]
    return (att_grad, in_grad, router_grad)


def solution(mesh):
    in_specs = (
        P("dp", "seq", "tensor"),
        P("dp", "seq"),
        P("dp", "seq", "tensor"),
        P("dp", "seq", "tensor"),
        P("tensor", None),
        P("tensor"),
        P("dp", "seq"),
        P("dp", None),
    )
    out_specs = (P("dp", "seq", "tensor"), P("dp", "seq", "tensor"), P("tensor"))
    return jax.shard_map(shards, mesh=mesh, in_specs=in_specs, out_specs=out_specs, check_vma=False)
```

```python
import functools
import math

import jax
import jax.numpy as jnp
from jax import lax
from jax.experimental import pallas as pl
from jax.experimental.pallas import tpu as pltpu
from jax.sharding import PartitionSpec as P


VMEM = pl.BlockSpec(memory_space=pltpu.VMEM)
SMEM = pl.BlockSpec(memory_space=pltpu.SMEM)
PARAMS = pltpu.CompilerParams(vmem_limit_bytes=32 * 1024 * 1024)


def pack_kernel(
    here_ref, counts_ref, keep_ref, att_any, slots_ref, ids_ref, places_ref, att_ref, att_sem
):
    fetch = pltpu.make_async_copy(att_any, att_ref, att_sem)
    fetch.start()
    nseq = counts_ref.shape[1]
    tok = keep_ref.shape[1]
    kept_rows = att_ref.shape[0]
    cap = tok // nseq
    seq_bits, cap_bits = nseq.bit_length() - 1, cap.bit_length() - 1
    here = here_ref[0]
    lane = lax.broadcasted_iota(jnp.int32, (1, tok), 1)
    block = lane >> cap_bits
    offset, own_offset = jnp.int32(0), jnp.int32(0)
    offsets = jnp.zeros((1, tok), jnp.int32)
    counts = jnp.zeros((1, tok), jnp.int32)
    for j in range(nseq):
        count = counts_ref[0, j]
        offsets = jnp.where(block == j, offset, offsets)
        counts = jnp.where(block == j, count, counts)
        own_offset = own_offset + jnp.where(j < here, count, 0)
        offset = offset + count
    order_in = ((here - offsets) & (nseq - 1)) + nseq * (lane & (cap - 1))
    places = jnp.where(order_in < counts, (offsets + order_in) >> seq_bits, -1)
    places_ref[...] = places

    keep = keep_ref[...]
    flags = jnp.broadcast_to(keep.astype(jnp.float32), (16, tok)).astype(jnp.bfloat16)
    upto = lax.broadcasted_iota(jnp.int32, (tok, tok), 0) <= lax.broadcasted_iota(
        jnp.int32, (tok, tok), 1
    )
    upto = jnp.where(upto, 1.0, 0.0).astype(jnp.bfloat16)
    sums = jnp.dot(flags, upto, preferred_element_type=jnp.float32)
    local = sums[0:1].astype(jnp.int32) - 1
    ranks = own_offset + local
    slot = (ranks & (nseq - 1)) * cap + (local >> seq_bits)
    ids_ref[...] = jnp.where(keep == 1, slot, -1)

    table = lax.broadcasted_iota(jnp.int32, (kept_rows, tok), 0) == places
    table = jnp.where(table, 1.0, 0.0).astype(jnp.bfloat16)
    fetch.wait()
    slots_ref[...] = lax.dot_general(
        table, att_ref[...], (((0,), (0,)), ((), ())), preferred_element_type=jnp.float32
    ).astype(jnp.bfloat16)


def rate_of(logits_ref):
    return jax.nn.sigmoid(logits_ref[...].astype(jnp.float32))


def finish_kernel(att_ref, ids_ref, logits_ref, back_ref, slots_ref, dots_ref):
    tok = ids_ref.shape[1]
    table = lax.broadcasted_iota(jnp.int32, (tok, tok), 0) == ids_ref[...]
    table = jnp.where(table, 1.0, 0.0).astype(jnp.bfloat16)
    att_tok = lax.dot_general(
        table, att_ref[...], (((0,), (0,)), ((), ())), preferred_element_type=jnp.float32
    )
    back = back_ref[...]
    column = jnp.sum(att_tok * back, axis=1, keepdims=True)
    dots_ref[...] = jnp.broadcast_to(column, (tok, 128)).T[0:1]
    rate = jnp.broadcast_to(rate_of(logits_ref), (128, tok)).T[:, 0:1]
    grad = (rate * back).astype(jnp.bfloat16)
    slots_ref[...] = jnp.dot(table, grad, preferred_element_type=jnp.float32).astype(jnp.bfloat16)


def router_kernel(scale, dots_ref, logits_ref, inputs_ref, copies_ref, grad_ref):
    rate = rate_of(logits_ref)
    grad = rate * (1.0 - rate) * dots_ref[...]
    grad_ref[...] = grad
    high = grad.astype(jnp.bfloat16).astype(jnp.float32)
    middle = (grad - high).astype(jnp.bfloat16).astype(jnp.float32)
    low = grad - high - middle
    row = lax.broadcasted_iota(jnp.int32, (16, grad.shape[1]), 0)
    parts = jnp.where(row == 0, high, jnp.where(row == 1, middle, jnp.where(row == 2, low, 0.0)))
    sums = jnp.dot(
        parts.astype(jnp.bfloat16), inputs_ref[...], preferred_element_type=jnp.float32
    )
    total = scale * jnp.sum(sums, axis=0, keepdims=True)
    copies_ref[...] = jnp.broadcast_to(total[None], copies_ref.shape)


def shards(
    inputs, logits, cotangent, attended, out_weight, router_weight, keep_route, shard_counts
):
    nseq = lax.axis_size("seq")
    here = lax.axis_index("seq")
    nten = lax.axis_size("tensor")
    column = lax.axis_index("tensor")
    batch, tok, width = cotangent.shape
    kept_rows = attended.shape[1]
    heads_width, model = out_weight.shape
    cap = tok // nseq
    scale = 1.0 / math.sqrt(model)

    flip = 1 - 2 * (here % 2)

    def turn(block, way):
        pairs = [
            (s * nten + i, s * nten + (i + (way if s % 2 == 0 else -way)) % nten)
            for s in range(nseq)
            for i in range(nten)
        ]
        return lax.ppermute(block, ("seq", "tensor"), pairs)

    def times(block, step):
        start = (column + step * flip) % nten * width
        weight = lax.dynamic_slice(out_weight, (0, start), (heads_width, width))
        return lax.dot_general(
            block, weight, (((1,), (1,)), ((), ())), preferred_element_type=jnp.float32
        )

    slots_shape = jax.ShapeDtypeStruct((tok, heads_width), jnp.bfloat16)
    row_shape = jax.ShapeDtypeStruct((1, tok), jnp.int32)
    att_slots, slot_ids, places = pl.pallas_call(
        pack_kernel,
        out_shape=(slots_shape, row_shape, row_shape),
        in_specs=[SMEM, SMEM, VMEM, pl.BlockSpec(memory_space=pl.ANY)],
        out_specs=(VMEM, VMEM, VMEM),
        scratch_shapes=[
            pltpu.VMEM((kept_rows, heads_width), jnp.bfloat16),
            pltpu.SemaphoreType.DMA,
        ],
        compiler_params=PARAMS,
        cost_estimate=pl.CostEstimate(
            flops=2 * tok * kept_rows * heads_width, bytes_accessed=2**20, transcendentals=0
        ),
    )(here.reshape(1), shard_counts, keep_route, attended[0])

    def exchange(slots):
        parts = slots.reshape(nseq, cap, slots.shape[1])
        moved = lax.all_to_all(parts, "seq", split_axis=0, concat_axis=0, tiled=True)
        return moved.reshape(tok, slots.shape[1])

    att_in = exchange(att_slots)

    own = cotangent[0]
    first_in, second_in = own, own
    product = None
    for step in range(1, nten // 2):
        first_in = turn(first_in, 1)
        second_in = turn(second_in, -1)
        if step == 1:
            own, first_in = lax.optimization_barrier((own, first_in))
            product = times(own, 0)
        product = product + times(first_in, -step) + times(second_in, step)
    last_in = turn(first_in, 1)
    product = product + times(last_in, nten // 2)

    grad_slots, partial_dots = pl.pallas_call(
        finish_kernel,
        out_shape=(slots_shape, jax.ShapeDtypeStruct((1, tok), jnp.float32)),
        in_specs=[VMEM] * 4,
        out_specs=(VMEM, VMEM),
        compiler_params=PARAMS,
        cost_estimate=pl.CostEstimate(
            flops=4 * tok * tok * heads_width, bytes_accessed=2**21, transcendentals=0
        ),
    )(att_in, slot_ids, logits, product)
    grad_in = exchange(grad_slots)
    dots = lax.psum(partial_dots, "tensor")
    group = lax.axis_size("dp") * nseq
    copies, logit_grad = pl.pallas_call(
        functools.partial(router_kernel, scale),
        out_shape=(
            jax.ShapeDtypeStruct((group, 1, width), jnp.float32),
            jax.ShapeDtypeStruct((1, tok), jnp.float32),
        ),
        in_specs=[VMEM] * 3,
        out_specs=(VMEM, VMEM),
        compiler_params=PARAMS,
        cost_estimate=pl.CostEstimate(
            flops=32 * tok * width, bytes_accessed=2**20, transcendentals=0
        ),
    )(dots, logits, inputs[0])
    grad_in, copies = lax.optimization_barrier((grad_in, copies))

    router_grad = jnp.sum(lax.all_to_all(copies, ("dp", "seq"), 0, 0, tiled=True), axis=(0, 1))
    in_grad = (
        cotangent.astype(jnp.float32)
        + scale * logit_grad[:, :, None] * router_weight[None, None, :]
    ).astype(jnp.bfloat16)
    place_table = (
        jnp.arange(kept_rows, dtype=jnp.int32)[:, None] == places
    ).astype(jnp.bfloat16)
    att_grad = jnp.dot(place_table, grad_in, preferred_element_type=jnp.float32)
    att_grad = att_grad.astype(jnp.bfloat16)[None]
    return (att_grad, in_grad, router_grad)


def solution(mesh):
    in_specs = (
        P("dp", "seq", "tensor"),
        P("dp", "seq"),
        P("dp", "seq", "tensor"),
        P("dp", "seq", "tensor"),
        P("tensor", None),
        P("tensor"),
        P("dp", "seq"),
        P("dp", None),
    )
    out_specs = (P("dp", "seq", "tensor"), P("dp", "seq", "tensor"), P("tensor"))
    return jax.shard_map(shards, mesh=mesh, in_specs=in_specs, out_specs=out_specs, check_vma=False)
```

```python
import functools
import math

import jax
import jax.numpy as jnp
from jax import lax
from jax.experimental import pallas as pl
from jax.experimental.pallas import tpu as pltpu
from jax.sharding import PartitionSpec as P


VMEM = pl.BlockSpec(memory_space=pltpu.VMEM)
SMEM = pl.BlockSpec(memory_space=pltpu.SMEM)
PARAMS = pltpu.CompilerParams(vmem_limit_bytes=32 * 1024 * 1024)


def table_kernel(here_ref, counts_ref, keep_ref, ids_ref, places_ref):
    nseq = counts_ref.shape[1]
    tok = keep_ref.shape[1]
    cap = tok // nseq
    seq_bits, cap_bits = nseq.bit_length() - 1, cap.bit_length() - 1
    here = here_ref[0]
    lane = lax.broadcasted_iota(jnp.int32, (1, tok), 1)
    block = lane >> cap_bits
    offset, own_offset = jnp.int32(0), jnp.int32(0)
    offsets = jnp.zeros((1, tok), jnp.int32)
    counts = jnp.zeros((1, tok), jnp.int32)
    for j in range(nseq):
        count = counts_ref[0, j]
        offsets = jnp.where(block == j, offset, offsets)
        counts = jnp.where(block == j, count, counts)
        own_offset = own_offset + jnp.where(j < here, count, 0)
        offset = offset + count
    order_in = ((here - offsets) & (nseq - 1)) + nseq * (lane & (cap - 1))
    places = jnp.where(order_in < counts, (offsets + order_in) >> seq_bits, -1)
    places_ref[...] = places

    keep = keep_ref[...]
    flags = jnp.broadcast_to(keep.astype(jnp.float32), (16, tok)).astype(jnp.bfloat16)
    upto = lax.broadcasted_iota(jnp.int32, (tok, tok), 0) <= lax.broadcasted_iota(
        jnp.int32, (tok, tok), 1
    )
    upto = jnp.where(upto, 1.0, 0.0).astype(jnp.bfloat16)
    sums = jnp.dot(flags, upto, preferred_element_type=jnp.float32)
    local = sums[0:1].astype(jnp.int32) - 1
    ranks = own_offset + local
    slot = (ranks & (nseq - 1)) * cap + (local >> seq_bits)
    ids_ref[...] = jnp.where(keep == 1, slot, -1)


def rate_of(logits_ref):
    return jax.nn.sigmoid(logits_ref[...].astype(jnp.float32))


def finish_kernel(att_ref, ids_ref, logits_ref, back_ref, slots_ref, dots_ref):
    tok = ids_ref.shape[1]
    table = lax.broadcasted_iota(jnp.int32, (tok, tok), 0) == ids_ref[...]
    table = jnp.where(table, 1.0, 0.0).astype(jnp.bfloat16)
    att_tok = lax.dot_general(
        table, att_ref[...], (((0,), (0,)), ((), ())), preferred_element_type=jnp.float32
    )
    back = back_ref[...]
    column = jnp.sum(att_tok * back, axis=1, keepdims=True)
    dots_ref[...] = jnp.broadcast_to(column, (tok, 128)).T[0:1]
    rate = jnp.broadcast_to(rate_of(logits_ref), (128, tok)).T[:, 0:1]
    grad = (rate * back).astype(jnp.bfloat16)
    slots_ref[...] = jnp.dot(table, grad, preferred_element_type=jnp.float32).astype(jnp.bfloat16)


def router_kernel(scale, dots_ref, logits_ref, inputs_ref, copies_ref, grad_ref):
    rate = rate_of(logits_ref)
    grad = rate * (1.0 - rate) * dots_ref[...]
    grad_ref[...] = grad
    high = grad.astype(jnp.bfloat16).astype(jnp.float32)
    middle = (grad - high).astype(jnp.bfloat16).astype(jnp.float32)
    low = grad - high - middle
    row = lax.broadcasted_iota(jnp.int32, (16, grad.shape[1]), 0)
    parts = jnp.where(row == 0, high, jnp.where(row == 1, middle, jnp.where(row == 2, low, 0.0)))
    sums = jnp.dot(
        parts.astype(jnp.bfloat16), inputs_ref[...], preferred_element_type=jnp.float32
    )
    total = scale * jnp.sum(sums, axis=0, keepdims=True)
    copies_ref[...] = jnp.broadcast_to(total[None], copies_ref.shape)


def shards(
    inputs, logits, cotangent, attended, out_weight, router_weight, keep_route, shard_counts
):
    nseq = lax.axis_size("seq")
    here = lax.axis_index("seq")
    nten = lax.axis_size("tensor")
    column = lax.axis_index("tensor")
    batch, tok, width = cotangent.shape
    kept_rows = attended.shape[1]
    heads_width, model = out_weight.shape
    cap = tok // nseq
    scale = 1.0 / math.sqrt(model)

    flip = 1 - 2 * (here % 2)

    def turn(block, way):
        pairs = [
            (s * nten + i, s * nten + (i + (way if s % 2 == 0 else -way)) % nten)
            for s in range(nseq)
            for i in range(nten)
        ]
        return lax.ppermute(block, ("seq", "tensor"), pairs)

    def weight_of(step):
        start = (column + step * flip) % nten * width
        return lax.dynamic_slice(out_weight, (0, start), (heads_width, width))

    def times(block, step, weight=None):
        weight = weight_of(step) if weight is None else weight
        return lax.dot_general(
            block, weight, (((1,), (1,)), ((), ())), preferred_element_type=jnp.float32
        )

    slots_shape = jax.ShapeDtypeStruct((tok, heads_width), jnp.bfloat16)
    row_shape = jax.ShapeDtypeStruct((1, tok), jnp.int32)
    slot_ids, places = pl.pallas_call(
        table_kernel,
        out_shape=(row_shape, row_shape),
        in_specs=[SMEM, SMEM, VMEM],
        out_specs=(VMEM, VMEM),
        compiler_params=PARAMS,
        cost_estimate=pl.CostEstimate(flops=32 * tok * tok, bytes_accessed=2**13, transcendentals=0),
    )(here.reshape(1), shard_counts, keep_route)
    place_table = (jnp.arange(kept_rows, dtype=jnp.int32)[:, None] == places).astype(jnp.bfloat16)

    def exchange(slots):
        parts = slots.reshape(nseq, cap, slots.shape[1])
        moved = lax.all_to_all(parts, "seq", split_axis=0, concat_axis=0, tiled=True)
        return moved.reshape(tok, slots.shape[1])

    own = cotangent[0]
    first_in, second_in = own, own
    product = None
    for step in range(1, nten // 2):
        first_in = turn(first_in, 1)
        second_in = turn(second_in, -1)
        if step == 1:
            own, first_in = lax.optimization_barrier((own, first_in))
            product = times(own, 0)
        if step == 2:
            att_rows, first_in = lax.optimization_barrier((attended[0], first_in))
            att_slots = lax.dot_general(
                place_table, att_rows, (((0,), (0,)), ((), ())), preferred_element_type=jnp.float32
            )
            att_in = exchange(att_slots.astype(jnp.bfloat16))
        product = product + times(first_in, -step) + times(second_in, step)
    last_in = turn(first_in, 1)
    last_weight = lax.optimization_barrier(weight_of(nten // 2))
    product = product + times(last_in, nten // 2, last_weight)

    grad_slots, partial_dots = pl.pallas_call(
        finish_kernel,
        out_shape=(slots_shape, jax.ShapeDtypeStruct((1, tok), jnp.float32)),
        in_specs=[VMEM] * 4,
        out_specs=(VMEM, VMEM),
        compiler_params=PARAMS,
        cost_estimate=pl.CostEstimate(
            flops=4 * tok * tok * heads_width, bytes_accessed=2**21, transcendentals=0
        ),
    )(att_in, slot_ids, logits, product)
    grad_in = exchange(grad_slots)
    dots = lax.psum(partial_dots, "tensor")
    group = lax.axis_size("dp") * nseq
    copies, logit_grad = pl.pallas_call(
        functools.partial(router_kernel, scale),
        out_shape=(
            jax.ShapeDtypeStruct((group, 1, width), jnp.float32),
            jax.ShapeDtypeStruct((1, tok), jnp.float32),
        ),
        in_specs=[VMEM] * 3,
        out_specs=(VMEM, VMEM),
        compiler_params=PARAMS,
        cost_estimate=pl.CostEstimate(
            flops=32 * tok * width, bytes_accessed=2**20, transcendentals=0
        ),
    )(dots, logits, inputs[0])
    grad_in, copies = lax.optimization_barrier((grad_in, copies))

    router_grad = jnp.sum(lax.all_to_all(copies, ("dp", "seq"), 0, 0, tiled=True), axis=(0, 1))
    in_grad = (
        cotangent.astype(jnp.float32)
        + scale * logit_grad[:, :, None] * router_weight[None, None, :]
    ).astype(jnp.bfloat16)
    att_grad = jnp.dot(place_table, grad_in, preferred_element_type=jnp.float32)
    att_grad = att_grad.astype(jnp.bfloat16)[None]
    return (att_grad, in_grad, router_grad)


def solution(mesh):
    in_specs = (
        P("dp", "seq", "tensor"),
        P("dp", "seq"),
        P("dp", "seq", "tensor"),
        P("dp", "seq", "tensor"),
        P("tensor", None),
        P("tensor"),
        P("dp", "seq"),
        P("dp", None),
    )
    out_specs = (P("dp", "seq", "tensor"), P("dp", "seq", "tensor"), P("tensor"))
    return jax.shard_map(shards, mesh=mesh, in_specs=in_specs, out_specs=out_specs, check_vma=False)
```

```python
import functools
import math

import jax
import jax.numpy as jnp
from jax import lax
from jax.experimental import pallas as pl
from jax.experimental.pallas import tpu as pltpu
from jax.sharding import PartitionSpec as P


VMEM = pl.BlockSpec(memory_space=pltpu.VMEM)
SMEM = pl.BlockSpec(memory_space=pltpu.SMEM)
PARAMS = pltpu.CompilerParams(vmem_limit_bytes=32 * 1024 * 1024)


def pack_kernel(
    here_ref, counts_ref, keep_ref, att_any, slots_ref, ids_ref, places_ref, att_ref, att_sem
):
    fetch = pltpu.make_async_copy(att_any, att_ref, att_sem)
    fetch.start()
    nseq = counts_ref.shape[1]
    tok = keep_ref.shape[1]
    kept_rows = att_ref.shape[0]
    cap = tok // nseq
    seq_bits, cap_bits = nseq.bit_length() - 1, cap.bit_length() - 1
    here = here_ref[0]
    lane = lax.broadcasted_iota(jnp.int32, (1, tok), 1)
    block = lane >> cap_bits
    offset, own_offset = jnp.int32(0), jnp.int32(0)
    offsets = jnp.zeros((1, tok), jnp.int32)
    counts = jnp.zeros((1, tok), jnp.int32)
    for j in range(nseq):
        count = counts_ref[0, j]
        offsets = jnp.where(block == j, offset, offsets)
        counts = jnp.where(block == j, count, counts)
        own_offset = own_offset + jnp.where(j < here, count, 0)
        offset = offset + count
    order_in = ((here - offsets) & (nseq - 1)) + nseq * (lane & (cap - 1))
    places = jnp.where(order_in < counts, (offsets + order_in) >> seq_bits, -1)
    places_ref[...] = places

    keep = keep_ref[...]
    flags = jnp.broadcast_to(keep.astype(jnp.float32), (16, tok)).astype(jnp.bfloat16)
    upto = lax.broadcasted_iota(jnp.int32, (tok, tok), 0) <= lax.broadcasted_iota(
        jnp.int32, (tok, tok), 1
    )
    upto = jnp.where(upto, 1.0, 0.0).astype(jnp.bfloat16)
    sums = jnp.dot(flags, upto, preferred_element_type=jnp.float32)
    local = sums[0:1].astype(jnp.int32) - 1
    ranks = own_offset + local
    slot = (ranks & (nseq - 1)) * cap + (local >> seq_bits)
    ids_ref[...] = jnp.where(keep == 1, slot, -1)

    table = lax.broadcasted_iota(jnp.int32, (kept_rows, tok), 0) == places
    table = jnp.where(table, 1.0, 0.0).astype(jnp.bfloat16)
    fetch.wait()
    slots_ref[...] = lax.dot_general(
        table, att_ref[...], (((0,), (0,)), ((), ())), preferred_element_type=jnp.float32
    ).astype(jnp.bfloat16)


def rate_of(logits_ref):
    return jax.nn.sigmoid(logits_ref[...].astype(jnp.float32))


def finish_kernel(
    att_ref, ids_ref, logits_ref, sum_ref, last_ref, weight_ref, slots_ref, dots_ref
):
    tok = ids_ref.shape[1]
    table = lax.broadcasted_iota(jnp.int32, (tok, tok), 0) == ids_ref[...]
    table = jnp.where(table, 1.0, 0.0).astype(jnp.bfloat16)
    att_tok = att_ref[...].astype(jnp.float32)
    back = sum_ref[...] + lax.dot_general(
        last_ref[...], weight_ref[...], (((1,), (1,)), ((), ())),
        preferred_element_type=jnp.float32,
    )
    column = jnp.sum(att_tok * back, axis=1, keepdims=True)
    dots_ref[...] = jnp.broadcast_to(column, (tok, 128)).T[0:1]
    rate = jnp.broadcast_to(rate_of(logits_ref), (128, tok)).T[:, 0:1]
    grad = (rate * back).astype(jnp.bfloat16)
    slots_ref[...] = jnp.dot(table, grad, preferred_element_type=jnp.float32).astype(jnp.bfloat16)


def router_kernel(scale, dots_ref, logits_ref, inputs_ref, copies_ref, grad_ref):
    rate = rate_of(logits_ref)
    grad = rate * (1.0 - rate) * dots_ref[...]
    grad_ref[...] = grad
    high = grad.astype(jnp.bfloat16).astype(jnp.float32)
    middle = (grad - high).astype(jnp.bfloat16).astype(jnp.float32)
    low = grad - high - middle
    row = lax.broadcasted_iota(jnp.int32, (16, grad.shape[1]), 0)
    parts = jnp.where(row == 0, high, jnp.where(row == 1, middle, jnp.where(row == 2, low, 0.0)))
    sums = jnp.dot(
        parts.astype(jnp.bfloat16), inputs_ref[...], preferred_element_type=jnp.float32
    )
    total = scale * jnp.sum(sums, axis=0, keepdims=True)
    copies_ref[...] = jnp.broadcast_to(total[None], copies_ref.shape)


def shards(
    inputs, logits, cotangent, attended, out_weight, router_weight, keep_route, shard_counts
):
    nseq = lax.axis_size("seq")
    here = lax.axis_index("seq")
    nten = lax.axis_size("tensor")
    column = lax.axis_index("tensor")
    batch, tok, width = cotangent.shape
    kept_rows = attended.shape[1]
    heads_width, model = out_weight.shape
    cap = tok // nseq
    scale = 1.0 / math.sqrt(model)

    flip = 1 - 2 * (here % 2)

    def turn(block, way):
        pairs = [
            (s * nten + i, s * nten + (i + (way if s % 2 == 0 else -way)) % nten)
            for s in range(nseq)
            for i in range(nten)
        ]
        return lax.ppermute(block, ("seq", "tensor"), pairs)

    def weight_of(step):
        start = (column + step * flip) % nten * width
        return lax.dynamic_slice(out_weight, (0, start), (heads_width, width))

    def times(block, step):
        return lax.dot_general(
            block, weight_of(step), (((1,), (1,)), ((), ())), preferred_element_type=jnp.float32
        )

    slots_shape = jax.ShapeDtypeStruct((tok, heads_width), jnp.bfloat16)
    row_shape = jax.ShapeDtypeStruct((1, tok), jnp.int32)
    att_slots, slot_ids, places = pl.pallas_call(
        pack_kernel,
        out_shape=(slots_shape, row_shape, row_shape),
        in_specs=[SMEM, SMEM, VMEM, pl.BlockSpec(memory_space=pl.ANY)],
        out_specs=(VMEM, VMEM, VMEM),
        scratch_shapes=[
            pltpu.VMEM((kept_rows, heads_width), jnp.bfloat16),
            pltpu.SemaphoreType.DMA,
        ],
        compiler_params=PARAMS,
        cost_estimate=pl.CostEstimate(
            flops=2 * tok * kept_rows * heads_width, bytes_accessed=2**20, transcendentals=0
        ),
    )(here.reshape(1), shard_counts, keep_route, attended[0])

    def exchange(slots):
        parts = slots.reshape(nseq, cap, slots.shape[1])
        moved = lax.all_to_all(parts, "seq", split_axis=0, concat_axis=0, tiled=True)
        return moved.reshape(tok, slots.shape[1])

    att_in = exchange(att_slots)

    own = cotangent[0]
    first_in, second_in = own, own
    product = None
    for step in range(1, nten // 2):
        first_in = turn(first_in, 1)
        second_in = turn(second_in, -1)
        if step == 1:
            own, first_in = lax.optimization_barrier((own, first_in))
            product = times(own, 0)
        product = product + times(first_in, -step) + times(second_in, step)
    last_in = turn(first_in, 1)
    slot_table = (jnp.arange(tok, dtype=jnp.int32)[:, None] == slot_ids).astype(jnp.bfloat16)
    att_tok = lax.dot_general(
        slot_table, att_in, (((0,), (0,)), ((), ())), preferred_element_type=jnp.float32
    ).astype(jnp.bfloat16)
    product, att_tok, last_weight = lax.optimization_barrier(
        (product, att_tok, weight_of(nten // 2))
    )

    grad_slots, partial_dots = pl.pallas_call(
        finish_kernel,
        out_shape=(slots_shape, jax.ShapeDtypeStruct((1, tok), jnp.float32)),
        in_specs=[VMEM] * 6,
        out_specs=(VMEM, VMEM),
        compiler_params=PARAMS,
        cost_estimate=pl.CostEstimate(
            flops=4 * tok * tok * heads_width, bytes_accessed=2**21, transcendentals=0
        ),
    )(att_tok, slot_ids, logits, product, last_in, last_weight)
    grad_in = exchange(grad_slots)
    dots = lax.psum(partial_dots, "tensor")
    group = lax.axis_size("dp") * nseq
    copies, logit_grad = pl.pallas_call(
        functools.partial(router_kernel, scale),
        out_shape=(
            jax.ShapeDtypeStruct((group, 1, width), jnp.float32),
            jax.ShapeDtypeStruct((1, tok), jnp.float32),
        ),
        in_specs=[VMEM] * 3,
        out_specs=(VMEM, VMEM),
        compiler_params=PARAMS,
        cost_estimate=pl.CostEstimate(
            flops=32 * tok * width, bytes_accessed=2**20, transcendentals=0
        ),
    )(dots, logits, inputs[0])
    grad_in, copies = lax.optimization_barrier((grad_in, copies))

    router_grad = jnp.sum(lax.all_to_all(copies, ("dp", "seq"), 0, 0, tiled=True), axis=(0, 1))
    in_grad = (
        cotangent.astype(jnp.float32)
        + scale * logit_grad[:, :, None] * router_weight[None, None, :]
    ).astype(jnp.bfloat16)
    place_table = (
        jnp.arange(kept_rows, dtype=jnp.int32)[:, None] == places
    ).astype(jnp.bfloat16)
    att_grad = jnp.dot(place_table, grad_in, preferred_element_type=jnp.float32)
    att_grad = att_grad.astype(jnp.bfloat16)[None]
    return (att_grad, in_grad, router_grad)


def solution(mesh):
    in_specs = (
        P("dp", "seq", "tensor"),
        P("dp", "seq"),
        P("dp", "seq", "tensor"),
        P("dp", "seq", "tensor"),
        P("tensor", None),
        P("tensor"),
        P("dp", "seq"),
        P("dp", None),
    )
    out_specs = (P("dp", "seq", "tensor"), P("dp", "seq", "tensor"), P("tensor"))
    return jax.shard_map(shards, mesh=mesh, in_specs=in_specs, out_specs=out_specs, check_vma=False)
```

```python
import functools
import math

import jax
import jax.numpy as jnp
from jax import lax
from jax.experimental import pallas as pl
from jax.experimental.pallas import tpu as pltpu
from jax.sharding import PartitionSpec as P


VMEM = pl.BlockSpec(memory_space=pltpu.VMEM)
SMEM = pl.BlockSpec(memory_space=pltpu.SMEM)
PARAMS = pltpu.CompilerParams(vmem_limit_bytes=32 * 1024 * 1024)


def pack_kernel(
    here_ref, counts_ref, keep_ref, att_any, slots_ref, ids_ref, places_ref, att_ref, att_sem
):
    fetch = pltpu.make_async_copy(att_any, att_ref, att_sem)
    fetch.start()
    nseq = counts_ref.shape[1]
    tok = keep_ref.shape[1]
    kept_rows = att_ref.shape[0]
    cap = tok // nseq
    seq_bits, cap_bits = nseq.bit_length() - 1, cap.bit_length() - 1
    here = here_ref[0]
    lane = lax.broadcasted_iota(jnp.int32, (1, tok), 1)
    block = lane >> cap_bits
    offset, own_offset = jnp.int32(0), jnp.int32(0)
    offsets = jnp.zeros((1, tok), jnp.int32)
    counts = jnp.zeros((1, tok), jnp.int32)
    for j in range(nseq):
        count = counts_ref[0, j]
        offsets = jnp.where(block == j, offset, offsets)
        counts = jnp.where(block == j, count, counts)
        own_offset = own_offset + jnp.where(j < here, count, 0)
        offset = offset + count
    order_in = ((here - offsets) & (nseq - 1)) + nseq * (lane & (cap - 1))
    places = jnp.where(order_in < counts, (offsets + order_in) >> seq_bits, -1)
    places_ref[...] = places

    keep = keep_ref[...]
    flags = jnp.broadcast_to(keep.astype(jnp.float32), (16, tok)).astype(jnp.bfloat16)
    upto = lax.broadcasted_iota(jnp.int32, (tok, tok), 0) <= lax.broadcasted_iota(
        jnp.int32, (tok, tok), 1
    )
    upto = jnp.where(upto, 1.0, 0.0).astype(jnp.bfloat16)
    sums = jnp.dot(flags, upto, preferred_element_type=jnp.float32)
    local = sums[0:1].astype(jnp.int32) - 1
    ranks = own_offset + local
    slot = (ranks & (nseq - 1)) * cap + (local >> seq_bits)
    ids_ref[...] = jnp.where(keep == 1, slot, -1)

    table = lax.broadcasted_iota(jnp.int32, (kept_rows, tok), 0) == places
    table = jnp.where(table, 1.0, 0.0).astype(jnp.bfloat16)
    fetch.wait()
    slots_ref[...] = lax.dot_general(
        table, att_ref[...], (((0,), (0,)), ((), ())), preferred_element_type=jnp.float32
    ).astype(jnp.bfloat16)


def rate_of(logits_ref):
    return jax.nn.sigmoid(logits_ref[...].astype(jnp.float32))


def finish_kernel(
    att_ref, ids_ref, logits_ref, sum_ref, last_ref, weight_ref, slots_ref, dots_ref
):
    tok = ids_ref.shape[1]
    table = lax.broadcasted_iota(jnp.int32, (tok, tok), 0) == ids_ref[...]
    table = jnp.where(table, 1.0, 0.0).astype(jnp.bfloat16)
    att_tok = att_ref[...].astype(jnp.float32)
    back = sum_ref[...] + lax.dot_general(
        last_ref[...], weight_ref[...], (((1,), (1,)), ((), ())),
        preferred_element_type=jnp.float32,
    )
    column = jnp.sum(att_tok * back, axis=1, keepdims=True)
    dots_ref[...] = jnp.broadcast_to(column, (tok, 128)).T[0:1]
    rate = jnp.broadcast_to(rate_of(logits_ref), (128, tok)).T[:, 0:1]
    grad = (rate * back).astype(jnp.bfloat16)
    slots_ref[...] = jnp.dot(table, grad, preferred_element_type=jnp.float32).astype(jnp.bfloat16)


def router_kernel(scale, dots_ref, logits_ref, inputs_ref, copies_ref, grad_ref):
    rate = rate_of(logits_ref)
    grad = rate * (1.0 - rate) * dots_ref[...]
    grad_ref[...] = grad
    high = grad.astype(jnp.bfloat16).astype(jnp.float32)
    middle = (grad - high).astype(jnp.bfloat16).astype(jnp.float32)
    low = grad - high - middle
    row = lax.broadcasted_iota(jnp.int32, (16, grad.shape[1]), 0)
    parts = jnp.where(row == 0, high, jnp.where(row == 1, middle, jnp.where(row == 2, low, 0.0)))
    sums = jnp.dot(
        parts.astype(jnp.bfloat16), inputs_ref[...], preferred_element_type=jnp.float32
    )
    total = scale * jnp.sum(sums, axis=0, keepdims=True)
    copies_ref[...] = jnp.broadcast_to(total[None], copies_ref.shape)


def shards(
    inputs, logits, cotangent, attended, out_weight, router_weight, keep_route, shard_counts
):
    nseq = lax.axis_size("seq")
    here = lax.axis_index("seq")
    nten = lax.axis_size("tensor")
    column = lax.axis_index("tensor")
    batch, tok, width = cotangent.shape
    kept_rows = attended.shape[1]
    heads_width, model = out_weight.shape
    cap = tok // nseq
    scale = 1.0 / math.sqrt(model)

    flip = 1 - 2 * (here % 2)

    def turn(block, way):
        pairs = [
            (s * nten + i, s * nten + (i + (way if s % 2 == 0 else -way)) % nten)
            for s in range(nseq)
            for i in range(nten)
        ]
        return lax.ppermute(block, ("seq", "tensor"), pairs)

    def weight_of(step, weight=out_weight):
        start = (column + step * flip) % nten * width
        return lax.dynamic_slice(weight, (0, start), (heads_width, width))

    def times(block, step):
        return lax.dot_general(
            block, weight_of(step), (((1,), (1,)), ((), ())), preferred_element_type=jnp.float32
        )

    slots_shape = jax.ShapeDtypeStruct((tok, heads_width), jnp.bfloat16)
    row_shape = jax.ShapeDtypeStruct((1, tok), jnp.int32)
    att_slots, slot_ids, places = pl.pallas_call(
        pack_kernel,
        out_shape=(slots_shape, row_shape, row_shape),
        in_specs=[SMEM, SMEM, VMEM, pl.BlockSpec(memory_space=pl.ANY)],
        out_specs=(VMEM, VMEM, VMEM),
        scratch_shapes=[
            pltpu.VMEM((kept_rows, heads_width), jnp.bfloat16),
            pltpu.SemaphoreType.DMA,
        ],
        compiler_params=PARAMS,
        cost_estimate=pl.CostEstimate(
            flops=2 * tok * kept_rows * heads_width, bytes_accessed=2**20, transcendentals=0
        ),
    )(here.reshape(1), shard_counts, keep_route, attended[0])

    def exchange(slots):
        parts = slots.reshape(nseq, cap, slots.shape[1])
        moved = lax.all_to_all(parts, "seq", split_axis=0, concat_axis=0, tiled=True)
        return moved.reshape(tok, slots.shape[1])

    att_in = exchange(att_slots)

    own = cotangent[0]
    first_in, second_in = own, own
    product = None
    for step in range(1, nten // 2):
        first_in = turn(first_in, 1)
        second_in = turn(second_in, -1)
        if step == 1:
            own, first_in = lax.optimization_barrier((own, first_in))
            product = times(own, 0)
        product = product + times(first_in, -step) + times(second_in, step)
    att_in, late_weight, first_in = lax.optimization_barrier((att_in, out_weight, first_in))
    last_in = turn(first_in, 1)
    slot_table = (jnp.arange(tok, dtype=jnp.int32)[:, None] == slot_ids).astype(jnp.bfloat16)
    att_tok = lax.dot_general(
        slot_table, att_in, (((0,), (0,)), ((), ())), preferred_element_type=jnp.float32
    ).astype(jnp.bfloat16)
    product, att_tok, last_weight = lax.optimization_barrier(
        (product, att_tok, weight_of(nten // 2, late_weight))
    )

    grad_slots, partial_dots = pl.pallas_call(
        finish_kernel,
        out_shape=(slots_shape, jax.ShapeDtypeStruct((1, tok), jnp.float32)),
        in_specs=[VMEM] * 6,
        out_specs=(VMEM, VMEM),
        compiler_params=PARAMS,
        cost_estimate=pl.CostEstimate(
            flops=4 * tok * tok * heads_width, bytes_accessed=2**21, transcendentals=0
        ),
    )(att_tok, slot_ids, logits, product, last_in, last_weight)
    grad_in = exchange(grad_slots)
    dots = lax.psum(partial_dots, "tensor")
    group = lax.axis_size("dp") * nseq
    copies, logit_grad = pl.pallas_call(
        functools.partial(router_kernel, scale),
        out_shape=(
            jax.ShapeDtypeStruct((group, 1, width), jnp.float32),
            jax.ShapeDtypeStruct((1, tok), jnp.float32),
        ),
        in_specs=[VMEM] * 3,
        out_specs=(VMEM, VMEM),
        compiler_params=PARAMS,
        cost_estimate=pl.CostEstimate(
            flops=32 * tok * width, bytes_accessed=2**20, transcendentals=0
        ),
    )(dots, logits, inputs[0])
    grad_in, copies = lax.optimization_barrier((grad_in, copies))

    router_grad = jnp.sum(lax.all_to_all(copies, ("dp", "seq"), 0, 0, tiled=True), axis=(0, 1))
    in_grad = (
        cotangent.astype(jnp.float32)
        + scale * logit_grad[:, :, None] * router_weight[None, None, :]
    ).astype(jnp.bfloat16)
    place_table = (
        jnp.arange(kept_rows, dtype=jnp.int32)[:, None] == places
    ).astype(jnp.bfloat16)
    att_grad = jnp.dot(place_table, grad_in, preferred_element_type=jnp.float32)
    att_grad = att_grad.astype(jnp.bfloat16)[None]
    return (att_grad, in_grad, router_grad)


def solution(mesh):
    in_specs = (
        P("dp", "seq", "tensor"),
        P("dp", "seq"),
        P("dp", "seq", "tensor"),
        P("dp", "seq", "tensor"),
        P("tensor", None),
        P("tensor"),
        P("dp", "seq"),
        P("dp", None),
    )
    out_specs = (P("dp", "seq", "tensor"), P("dp", "seq", "tensor"), P("tensor"))
    return jax.shard_map(shards, mesh=mesh, in_specs=in_specs, out_specs=out_specs, check_vma=False)
```
